256 devices in a mesh: row: 16 (over z, x_lo), col: 16 (over x_hi, y, core).
Axes of the slice: x: 4 (x_hi: 2, x_lo: 2; x = x_hi * 2 + x_lo), y: 4, z: 8, core: 2. Of those that a mesh axis runs over, the one named last changes fastest.
Arguments:
- cotangent: bfloat16 [2048, 8192], P('col', 'row'), may hold values from -6 to 6
- activations: bfloat16 [2048, 16384], P('row', 'col'), may hold values from -0.125 to 0.125
- down_weight: bfloat16 [16384, 8192], P('col', 'row'), may hold values from -0.046875 to 0.046875
- left_stats: float32 [16, 8192, 1024], P('col', 'row'), may hold values from -6 to 6
- right_stats: float32 [16, 8192, 1024], P('col', 'row'), may hold values from -6 to 6
- left_root: bfloat16 [16, 8192, 1024], P('col', 'row'), may hold values from -0.1875 to 0.1875
- right_root: bfloat16 [16, 1024, 8192], P('col', None, 'row'), may hold values from -0.1875 to 0.1875
Outputs:
- input_grad: bfloat16 [2048, 16384], P('row', 'col')
- update: bfloat16 [16384, 8192], P('col', 'row')
- left_new: float32 [16, 8192, 1024], P('col', 'row')
- right_new: float32 [16, 8192, 1024], P('col', 'row')
The draws below stay inside these ranges and needn't reach their ends.
All inputs are finite; a program needn't handle non-finite values.
Results may differ from the reference program's by a relative error of at most 0.0057.
Values may be sent and summed in bfloat16 or wider, within the bound.
No kernel may reach another device: no remote copies, remote signals or barrier semaphores. Data moves between devices by JAX's collectives and lax.ppermute only.
A program may use at most 128 MiB of HBM per device.

```python
import jax
import jax.numpy as jnp
from jax import lax

D = 8192
FF = 16384
BLOCK = 1024
TOKENS = 2048


def spiked(result, key, source, target, blocks, factor):
    owner, partner = [(jnp.arange(result.shape[axis_at]) // (result.shape[axis_at] // blocks)).reshape([-1 if axis == axis_at else 1 for axis in range(result.ndim)]) for axis_at in (source, target)]
    chosen = jax.random.permutation(key, blocks)[partner]
    strong = (owner == chosen) | (owner == (partner + blocks // 2) % blocks)
    return jnp.where(strong, factor * result, result)


def level_of(stream_key, extent, shards, least, top_value):
    factor_of, own = 1.0, jax.random.fold_in(stream_key, 6)
    for dim, blocks in shards:
        draws = jnp.exp(jax.random.uniform(jax.random.fold_in(own, dim), (blocks,), jnp.float32, least / len(shards), top_value / len(shards)))
        factor_of = factor_of * jnp.repeat(draws, extent[dim] // blocks).reshape([-1 if axis == dim else 1 for axis in range(len(extent))])
    return factor_of


def noise(key, dims, spread, bound, split=(), dtype=jnp.bfloat16):
    factor_of = level_of(key, dims, split, -0.22, 0.18) if split else 1.0
    array = jax.random.normal(key, dims, jnp.float32) * spread * factor_of
    return jnp.minimum(jnp.maximum(array, -bound), bound).astype(dtype)


def noise_with(key, extent, scale, most, pieces, heavy, held_as=jnp.bfloat16):
    values = scale * jax.random.normal(key, extent, jnp.float32)
    if pieces:
        values = values * level_of(key, extent, pieces, -0.22, 0.18)
    return jnp.clip(spiked(values, jax.random.fold_in(key, 3), *heavy), -most, most).astype(held_as)


def setup_inputs(seed: int = 0) -> dict:
    key_of = jax.random.split(jax.random.key(seed), 8)
    cotangent = noise_with(key_of[0], (TOKENS, D), 1.0, 6.0, ((0, 16), (1, 16)), (1, 0, 16, 2.0))
    activations = noise(key_of[1], (TOKENS, FF), TOKENS ** -0.5, 0.125, ((0, 16), (1, 16)))
    down_weight = noise(key_of[2], (FF, D), FF ** -0.5, 0.046875, ((0, 16), (1, 16)))
    left_stats = noise(key_of[3], (FF // BLOCK, D, BLOCK), 1.0, 6.0, ((0, 16), (1, 16)), jnp.float32)
    right_stats = noise(key_of[4], (FF // BLOCK, D, BLOCK), 1.0, 6.0, ((0, 16), (1, 16)), jnp.float32)
    left_root = noise(key_of[5], (FF // BLOCK, D, BLOCK), BLOCK ** -0.5, 0.1875, ((0, 16), (1, 16)))
    right_root = noise(key_of[6], (FF // BLOCK, BLOCK, D), BLOCK ** -0.5, 0.1875, ((0, 16), (2, 16)))
    return {"cotangent": cotangent, "activations": activations, "down_weight": down_weight, "left_stats": left_stats, "right_stats": right_stats, "left_root": left_root, "right_root": right_root}


def block_step(operands):
    grad_block, left_old, right_old, left_inv, right_inv = operands
    left_gram = jnp.dot(grad_block, grad_block.T, preferred_element_type=jnp.float32) / BLOCK
    right_gram = jnp.dot(grad_block.T, grad_block, preferred_element_type=jnp.float32) / BLOCK
    conditioned = jnp.dot(left_inv, grad_block, preferred_element_type=jnp.float32).astype(jnp.bfloat16)
    update_block = jnp.dot(conditioned, right_inv, preferred_element_type=jnp.float32).astype(jnp.bfloat16)
    return left_old + left_gram, right_old + right_gram, update_block


def reference(cotangent, activations, down_weight, left_stats, right_stats, left_root, right_root):
    gradient = jnp.dot(activations.T, cotangent, preferred_element_type=jnp.float32).astype(jnp.bfloat16)
    input_grad = jnp.dot(cotangent, down_weight.T, preferred_element_type=jnp.float32).astype(jnp.bfloat16)
    row_blocks = FF // BLOCK
    col_blocks = D // BLOCK

    def to_tiles(matrix):
        shaped = matrix.reshape(row_blocks, BLOCK, col_blocks, BLOCK)
        return shaped.transpose(0, 2, 1, 3).reshape(row_blocks * col_blocks, BLOCK, BLOCK)

    grad_tiles = to_tiles(gradient)
    left_tiles = left_stats.reshape(row_blocks * col_blocks, BLOCK, BLOCK)
    right_tiles = right_stats.reshape(row_blocks * col_blocks, BLOCK, BLOCK)
    left_inv = left_root.reshape(row_blocks * col_blocks, BLOCK, BLOCK)
    right_inv = to_tiles(right_root.reshape(row_blocks * BLOCK, D))
    left_out, right_out, update_tiles = lax.map(block_step, (grad_tiles, left_tiles, right_tiles, left_inv, right_inv))
    update = update_tiles.reshape(row_blocks, col_blocks, BLOCK, BLOCK).transpose(0, 2, 1, 3).reshape(FF, D)
    return (input_grad, update, left_out.reshape(row_blocks, D, BLOCK), right_out.reshape(row_blocks, D, BLOCK))
```

```python
import jax
import jax.numpy as jnp
from jax import lax
from jax.sharding import Mesh, PartitionSpec as P

F32 = jnp.float32
BF16 = jnp.bfloat16


def after(value, *others):
    return lax.optimization_barrier((value, *others))[0]


def swap(value, axis):
    return lax.ppermute(value, axis, [(0, 1), (1, 0)])


def shift(value, axis, distance):
    n = lax.axis_size(axis)
    return lax.ppermute(value, axis, [(i, (i + distance) % n) for i in range(n)])


def cross(value):
    return lax.ppermute(value, ("xl", "xh"), [(0, 3), (3, 0), (1, 2), (2, 1)])


def half(value, index, dim):
    size = value.shape[dim] // 2
    return lax.dynamic_slice_in_dim(value, index * size, size, dim)


def dot(a, b, contract):
    return lax.dot_general(a, b, ((contract[:1], contract[1:]), ((), ())), preferred_element_type=F32)


def order(h, own, other, dim):
    low = jnp.where(h == 0, own, other)
    high = jnp.where(h == 0, other, own)
    return jnp.concatenate([low, high], axis=dim)


def gather_z(block):
    n = lax.axis_size("z")
    z = lax.axis_index("z")
    out = jnp.zeros((n, *block.shape), block.dtype)
    out = lax.dynamic_update_index_in_dim(out, block, z, 0)
    up = down = block
    for step in range(1, n // 2 + 1):
        up = shift(up, "z", 1)
        out = lax.dynamic_update_index_in_dim(out, up, (z - step) % n, 0)
        if step < n // 2:
            down = shift(down, "z", -1)
            out = lax.dynamic_update_index_in_dim(out, down, (z + step) % n, 0)
    return out


def scatter_z(parts):
    n = lax.axis_size("z")
    z = lax.axis_index("z")
    rows = parts.shape[1]
    far = n // 2

    def part(k):
        return lax.dynamic_index_in_dim(parts, (z + k) % n, 0, keepdims=False)

    opposite = part(far)
    up = shift(opposite[: rows // 2].astype(BF16), "z", 1)
    down = shift(opposite[rows // 2 :].astype(BF16), "z", -1)
    up = jnp.pad(up, ((0, rows // 2), (0, 0)))
    down = jnp.pad(down, ((rows // 2, 0), (0, 0)))
    for k in range(far - 1, 0, -1):
        up = shift((part(k) + up.astype(F32)).astype(BF16), "z", 1)
        down = shift((part(-k) + down.astype(F32)).astype(BF16), "z", -1)
    return part(0) + up.astype(F32) + down.astype(F32)


def local(cotangent, activations, down_weight, left_stats, right_stats, left_root, right_root):
    h = lax.axis_index("xl")
    xh = lax.axis_index("xh")
    y = lax.axis_index("y")
    core = lax.axis_index("core")
    tok, d = cotangent.shape
    block = left_root.shape[2]
    left_stats, right_stats, left_root, right_root = (
        v[0] for v in (left_stats, right_stats, left_root, right_root)
    )

    act_other = swap(half(activations, 1 - h, 1), "xl")
    cot_pair = swap(cotangent, "xl")
    cot_cross = cross(cotangent)
    cot_far = swap(cotangent, "xh")
    act_two = order(h, half(activations, h, 1), act_other, 0)
    near = order(h, cotangent, cot_pair, 1)
    far = order(h, cot_far, cot_cross, 1)
    cot_x = jnp.stack([jnp.where(xh == 0, near, far), jnp.where(xh == 0, far, near)])

    act_all = gather_z(act_two).reshape(-1, d)
    y_up = shift(cot_x, "y", 1)
    y_down = shift(cot_x, "y", -1)
    y_far_0 = shift(y_up[0], "y", 1)
    y_far_1 = shift(y_down[1], "y", -1)
    cot_y = jnp.zeros((2, 4, tok, 2 * d), BF16)
    for k, v in ((0, cot_x), (-1, y_up), (1, y_down), (2, jnp.stack([y_far_0, y_far_1]))):
        cot_y = lax.dynamic_update_index_in_dim(cot_y, v, (y + k) % 4, 1)
    cot_c = swap(cot_y, "core")
    cot_all = jnp.stack(
        [jnp.where(core == 0, cot_y, cot_c), jnp.where(core == 0, cot_c, cot_y)], axis=2
    ).reshape(-1, 2 * d)

    weight_other = swap(half(down_weight, 1 - h, 0), "xl")
    weight = order(h, half(down_weight, h, 0), weight_other, 1)
    root_other = swap(left_root, "xl")

    grad = dot(act_all, cot_all, (0, 0)).astype(BF16)
    grad_other = swap(grad, "xl")

    parts = dot(cot_all, weight, (1, 1)).reshape(-1, 2 * tok, d)
    total = scatter_z(parts)
    keep = half(total, h, 0).astype(BF16)
    other = swap(half(total, 1 - h, 0).astype(BF16), "xl")
    input_grad = order(h, keep, other, 1)

    scale = 1.0 / block
    left_gram = order(h, dot(grad, grad, (1, 1)), dot(grad, grad_other, (1, 1)), 1)
    left_new = left_stats + left_gram * scale
    right_gram = dot(half(grad, h, 1), grad, (0, 0)) + dot(half(grad_other, h, 1), grad_other, (0, 0))
    right_new = right_stats + right_gram * scale

    m_own = dot(grad, right_root, (1, 0)).astype(BF16)
    m_other = dot(grad_other, right_root, (1, 0)).astype(BF16)
    m = order(h, m_own, m_other, 0)
    up_own = dot(left_root, m, (1, 0)).astype(BF16)
    up_other = dot(root_other, m, (1, 0)).astype(BF16)
    update = order(h, up_own, up_other, 0)
    return input_grad, update, left_new[None], right_new[None]


def solution(mesh):
    fine = Mesh(mesh.devices.reshape(8, 2, 2, 4, 2), ("z", "xl", "xh", "y", "core"))
    row, col = ("z", "xl"), ("xh", "y", "core")
    in_specs = (
        P(col, row),
        P(row, col),
        P(col, row),
        P(col, row, None),
        P(col, row, None),
        P(col, row, None),
        P(col, None, row),
    )
    out_specs = (P(row, col), P(col, row), P(col, row, None), P(col, row, None))
    return jax.shard_map(local, mesh=fine, in_specs=in_specs, out_specs=out_specs, check_vma=False)
```

```python
import jax
import jax.numpy as jnp
from jax import lax
from jax.experimental import pallas as pl
from jax.experimental.pallas import tpu as pltpu
from jax.sharding import Mesh, PartitionSpec as P

F32 = jnp.float32
BF16 = jnp.bfloat16
VMEM = pl.BlockSpec(memory_space=pltpu.VMEM)
SMEM = pl.BlockSpec(memory_space=pltpu.SMEM)
ANY = pl.BlockSpec(memory_space=pl.ANY)
PARAMS = pltpu.CompilerParams(vmem_limit_bytes=28 * 1024 * 1024)


def after(value, *others):
    return lax.optimization_barrier((value, *others))[0]


def swap(value, axis):
    return lax.ppermute(value, axis, [(0, 1), (1, 0)])


def step(value, axis):
    n = lax.axis_size(axis)
    pairs = [(2 * i + c, (i + 1 - 2 * c) % n * 2 + c) for i in range(n) for c in range(2)]
    return lax.ppermute(value, (axis, "core"), pairs)


def cross(value):
    return lax.ppermute(value, ("xl", "xh"), [(0, 3), (3, 0), (1, 2), (2, 1)])


def half(value, index, dim):
    size = value.shape[dim] // 2
    return lax.dynamic_slice_in_dim(value, index * size, size, dim)


def dot(a, b, contract):
    return lax.dot_general(a, b, ((contract[:1], contract[1:]), ((), ())), preferred_element_type=F32)


def order(h, own, other, dim):
    low = jnp.where(h == 0, own, other)
    high = jnp.where(h == 0, other, own)
    return jnp.concatenate([low, high], axis=dim)


def call(kernel, shapes, *args, specs=None, outs=None, scratch=()):
    return pl.pallas_call(
        kernel,
        out_shape=[jax.ShapeDtypeStruct(s, t) for s, t in shapes],
        in_specs=[SMEM] + (specs or [VMEM] * (len(args) - 1)),
        out_specs=outs or [VMEM] * len(shapes),
        scratch_shapes=list(scratch),
        compiler_params=PARAMS,
        cost_estimate=pl.CostEstimate(flops=0, bytes_accessed=0, transcendentals=0),
    )(*args)


def fetch(y_at, x_at, pieces, tokens, sems):
    tok = pieces[0].shape[1]
    for k in range(4):

        @pl.when(y_at == k)
        def _(k=k):
            for side in range(2):
                target = tokens.at[pl.ds(side * tok, tok)]
                pltpu.make_async_copy(pieces[2 * k + side].at[x_at], target, sems.at[side]).start()


def fetched(pieces, tokens, sems):
    tok = pieces[0].shape[1]
    for side in range(2):
        target = tokens.at[pl.ds(side * tok, tok)]
        pltpu.make_async_copy(pieces[side].at[0], target, sems.at[side]).wait()


def far_kernel(index, *refs):
    pieces, (weight, out, tokens, sems) = refs[:8], refs[8:]
    fetch(index[0], index[1], pieces, tokens, sems)
    fetched(pieces, tokens, sems)
    out[...] = dot(tokens[...], weight[...], (1, 1)).astype(BF16)


def part_kernel(index, *refs):
    pieces, (weight, sibling, *outs), (tokens, sems) = refs[:8], refs[8:14], refs[14:]
    for k in range(4):
        fetch(index[2 * k], index[2 * k + 1], pieces, tokens.at[k], sems.at[k])
    for k, out in enumerate(outs):
        fetched(pieces, tokens.at[k], sems.at[k])
        out[0] = dot(tokens[k], weight[...], (1, 1))
        if k < 3:
            out[1] = dot(tokens[k], sibling[...], (1, 1))


PICKS = (None, 0, 0, 0, 1, 1, 1, None)


def grad_kernel(index, *refs):
    acts, pieces = refs[:8], refs[8:16]
    out, rows, tokens, total, row_sems, sems = refs[16:]
    copies = []
    for k, pick in enumerate(PICKS):
        source = acts[k] if pick is None else acts[k].at[pick]
        copies.append(pltpu.make_async_copy(source, rows.at[k], row_sems.at[k]))
        copies[k].start()
        fetch(index[2 * k], index[2 * k + 1], pieces, tokens.at[k], sems.at[k])
    for k in range(8):
        copies[k].wait()
        fetched(pieces, tokens.at[k], sems.at[k])
        product = dot(rows[k], tokens[k], (0, 0))
        if k == 0:
            total[...] = product
        elif k < 7:
            total[...] += product
        else:
            out[...] = (total[...] + product).astype(BF16)


def own_kernel(index, grad, right_root, left_root, left_root_other, left_out, right_out, up_out):
    h = index[0]
    d = grad.shape[0]
    scale = 1.0 / (2 * d)
    at = pl.ds(pl.multiple_of(h * d, d), d)
    there = pl.ds(pl.multiple_of((1 - h) * d, d), d)
    left_out[...] = dot(grad[...], grad[...], (1, 1)) * scale
    right_out[...] = dot(grad[:, :d], grad[...], (0, 0)) * scale
    m = (dot(grad[:, :d], right_root[at], (1, 0)) + dot(grad[:, d:], right_root[there], (1, 0))).astype(BF16)
    up_out[:d] = dot(left_root[:, at], m, (1, 0))
    up_out[d:] = dot(left_root_other[:, at], m, (1, 0))


def other_kernel(index, *refs):
    (grad, other, right_root, left_root, left_root_other, left_own, right_own, up_own) = refs[:8]
    left_stats, right_stats, left_new, right_new, update = refs[8:13]
    left_in, right_in, left_buf, right_buf, up_buf, sems = refs[13:]
    h = index[0]
    d = grad.shape[0]
    scale = 1.0 / (2 * d)
    at = pl.ds(pl.multiple_of(h * d, d), d)
    there = pl.ds(pl.multiple_of((1 - h) * d, d), d)
    copy = pltpu.make_async_copy
    ins = [copy(left_stats, left_in, sems.at[0]), copy(right_stats, right_in, sems.at[1])]
    outs = [
        copy(up_buf, update, sems.at[2]),
        copy(left_buf, left_new, sems.at[3]),
        copy(right_buf, right_new, sems.at[4]),
    ]
    for c in ins:
        c.start()
    m = dot(other[:, d:], right_root[at], (1, 0)) + dot(other[:, :d], right_root[there], (1, 0))
    m = m.astype(BF16)
    up_buf[at] = (up_own[:d] + dot(left_root[:, there], m, (1, 0))).astype(BF16)
    up_buf[there] = (up_own[d:] + dot(left_root_other[:, there], m, (1, 0))).astype(BF16)
    outs[0].start()
    gram = dot(grad[:, :d], other[:, d:], (1, 1)) + dot(grad[:, d:], other[:, :d], (1, 1))
    ins[0].wait()
    left_buf[:, at] = left_in[:, at] + left_own[...]
    left_buf[:, there] = left_in[:, there] + gram * scale
    outs[1].start()
    mine = other[:, d:]
    gram = dot(mine, other[:, d:], (0, 0))
    ins[1].wait()
    right_buf[:, at] = right_in[:, at] + right_own[:, :d] + gram * scale
    gram = dot(mine, other[:, :d], (0, 0))
    right_buf[:, there] = right_in[:, there] + right_own[:, d:] + gram * scale
    outs[2].start()
    for c in outs:
        c.wait()


def cot_kernel(index, own, pair, far, cross_block, out):
    tok, d = own.shape
    out[0, :, :d] = own[...]
    out[0, :, d:] = pair[tok:]
    out[1, :, :d] = far[...]
    out[1, :, d:] = cross_block[...]


def send_kernel(index, act, own, out, sems):
    tok, d = own.shape
    at = pl.ds(pl.multiple_of(index[0] * d, d), d)
    copies = [
        pltpu.make_async_copy(act.at[:, at], out.at[pl.ds(0, tok)], sems.at[0]),
        pltpu.make_async_copy(own, out.at[pl.ds(tok, tok)], sems.at[1]),
    ]
    for c in copies:
        c.start()
    for c in copies:
        c.wait()


def add_kernel(index, part, arrived, out):
    if len(arrived.shape) == 2:
        out[0] = (part[0] + arrived[...].astype(F32)).astype(BF16)
        out[1] = part[1].astype(BF16)
    else:
        out[...] = (part[...] + arrived[...].astype(F32)).astype(BF16)


def last_kernel(index, part, arrived, sibling, keep, send):
    h = index[0]
    rows = keep.shape[0]

    def total(k):
        at = pl.ds(pl.multiple_of(k * rows, rows), rows)
        there = pl.ds(pl.multiple_of((1 - k) * rows, rows), rows)
        return part[0, at] + arrived[0, at].astype(F32) + sibling[1, there].astype(F32)

    keep[...] = total(h).astype(BF16)
    send[...] = total(1 - h).astype(BF16)


def local(cotangent, activations, down_weight, left_stats, right_stats, left_root, right_root):
    z = lax.axis_index("z")
    h = lax.axis_index("xl")
    xh = lax.axis_index("xh")
    y = lax.axis_index("y")
    core = lax.axis_index("core")
    sign = 1 - 2 * core
    tok, d = cotangent.shape
    block = left_root.shape[2]
    left_stats, right_stats, left_root, right_root = (
        v[0] for v in (left_stats, right_stats, left_root, right_root)
    )

    nothing = jnp.zeros((1,), jnp.int32)

    both = call(
        send_kernel,
        [((2 * tok, d), BF16)],
        (1 - h)[None],
        activations,
        cotangent,
        specs=[ANY] * 2,
        scratch=[pltpu.SemaphoreType.DMA((2,))],
    )[0]
    both = swap(both, "xl")
    cot_cross = cross(cotangent)
    cot_far = swap(cotangent, "xh")
    act = order(h ^ core, half(activations, h, 1), both[:tok], 0)
    cot = call(cot_kernel, [((2, tok, 2 * d), BF16)], nothing, cotangent, both, cot_far, cot_cross)[0]

    cot_s = swap(cot, "core")
    y_a = step(cot, "y")
    y_b = step(cot_s, "y")
    z_0 = jnp.stack([act, swap(act, "core")])
    z_1 = step(z_0, "z")
    z_2 = step(z_1, "z")
    z_3 = step(z_2, "z")
    z_4 = step(z_3[0], "z")
    s_1, s_2, s_3 = (swap(v, "core") for v in (z_1, z_2, z_3))

    weight_other = swap(half(down_weight, 1 - h, 0), "xl")
    weight = jnp.concatenate([half(down_weight, h, 0), weight_other], 1)
    weight_s = swap(weight, "core")
    root_after = after(left_root, weight_other)
    root_a = swap(root_after[: d // 2], "xl")
    root_b = swap(root_after[d // 2 :], "xl")

    y_c = step(y_a, "y")
    t_a, t_b, t_c = (swap(v, "core") for v in (y_a, y_b, y_c))
    pieces = (cot, cot_s, y_a, y_b, t_b, t_a, y_c, t_c)

    def place(k):
        target = (z + k * sign) % 8
        offset = (target % 4 - y) * sign % 4
        y_at = jnp.where(offset == 0, 0, jnp.where(offset == 3, 1, jnp.where(offset == 1, 2, 3)))
        return jnp.stack([y_at, xh ^ (target // 4)])

    def places(*ks):
        return jnp.concatenate([place(k) for k in ks])

    sem = pltpu.SemaphoreType.DMA
    grad = call(
        grad_kernel,
        [((d, 2 * d), BF16)],
        after(places(0, -1, -2, -3, 1, 2, 3, 4), root_b),
        act, z_1, z_2, z_3, s_1, s_2, s_3, z_4,
        *pieces,
        specs=[ANY] * 16,
        scratch=[
            pltpu.VMEM((8, 2 * tok, d), BF16),
            pltpu.VMEM((8, 2 * tok, 2 * d), BF16),
            pltpu.VMEM((d, 2 * d), F32),
            sem((8,)),
            sem((8, 2)),
        ],
    )[0]
    other = swap(grad, "xl")

    flow = call(
        far_kernel,
        [((2 * tok, d), BF16)],
        after(place(4), root_a),
        *pieces,
        weight,
        specs=[ANY] * 8 + [VMEM],
        scratch=[pltpu.VMEM((2 * tok, 2 * d), BF16), sem((2,))],
    )[0]
    flow = step(flow, "z")
    *parts, part_0 = call(
        part_kernel,
        [((2, 2 * tok, d), F32)] * 3 + [((1, 2 * tok, d), F32)],
        places(3, 2, 1, 0),
        *pieces,
        weight,
        weight_s,
        specs=[ANY] * 8 + [VMEM] * 2,
        scratch=[pltpu.VMEM((4, 2 * tok, 2 * d), BF16), sem((4, 2))],
    )
    for k, part in enumerate(parts):
        flow = call(add_kernel, [((2, 2 * tok, d), BF16)], nothing, part, flow)[0]
        if k < 2:
            flow = step(flow, "z")
    flow = step(flow, "z")
    keep, send = call(
        last_kernel, [((tok, d), BF16)] * 2, (h ^ core)[None], part_0, flow, swap(flow, "core")
    )
    input_grad = order(h, keep, swap(send, "xl"), 1)

    root_other = jnp.concatenate([root_a, root_b], 0)
    left_own, right_own, up_own = call(
        own_kernel,
        [((d, d), F32), ((d, 2 * d), F32), ((2 * d, d), F32)],
        h[None],
        grad,
        right_root,
        left_root,
        root_other,
    )
    stats = ((d, 2 * d), F32)
    left_new, right_new, update = call(
        other_kernel,
        [stats, stats, ((2 * d, d), BF16)],
        h[None],
        grad,
        other,
        right_root,
        left_root,
        root_other,
        left_own,
        right_own,
        up_own,
        left_stats,
        right_stats,
        specs=[VMEM] * 8 + [ANY] * 2,
        outs=[ANY] * 3,
        scratch=[pltpu.VMEM((d, 2 * d), F32)] * 4 + [pltpu.VMEM((2 * d, d), BF16), sem((5,))],
    )
    return input_grad, update, left_new[None], right_new[None]


def solution(mesh):
    fine = Mesh(mesh.devices.reshape(8, 2, 2, 4, 2), ("z", "xl", "xh", "y", "core"))
    row, col = ("z", "xl"), ("xh", "y", "core")
    in_specs = (
        P(col, row),
        P(row, col),
        P(col, row),
        P(col, row, None),
        P(col, row, None),
        P(col, row, None),
        P(col, None, row),
    )
    out_specs = (P(row, col), P(col, row), P(col, row, None), P(col, row, None))
    return jax.shard_map(local, mesh=fine, in_specs=in_specs, out_specs=out_specs, check_vma=False)
```

```python
import jax
import jax.numpy as jnp
from jax import lax
from jax.experimental import pallas as pl
from jax.experimental.pallas import tpu as pltpu
from jax.sharding import Mesh, PartitionSpec as P

F32 = jnp.float32
BF16 = jnp.bfloat16
VMEM = pl.BlockSpec(memory_space=pltpu.VMEM)
SMEM = pl.BlockSpec(memory_space=pltpu.SMEM)
ANY = pl.BlockSpec(memory_space=pl.ANY)
PARAMS = pltpu.CompilerParams(vmem_limit_bytes=40 * 1024 * 1024)


def after(value, *others):
    return lax.optimization_barrier((value, *others))[0]


def swap(value, axis):
    return lax.ppermute(value, axis, [(0, 1), (1, 0)])


def shift(value, axis, distance):
    n = lax.axis_size(axis)
    return lax.ppermute(value, axis, [(i, (i + distance) % n) for i in range(n)])


def cross(value):
    return lax.ppermute(value, ("xl", "xh"), [(0, 3), (3, 0), (1, 2), (2, 1)])


def half(value, index, dim):
    size = value.shape[dim] // 2
    return lax.dynamic_slice_in_dim(value, index * size, size, dim)


def dot(a, b, contract):
    return lax.dot_general(a, b, ((contract[:1], contract[1:]), ((), ())), preferred_element_type=F32)


def order(h, own, other, dim):
    low = jnp.where(h == 0, own, other)
    high = jnp.where(h == 0, other, own)
    return jnp.concatenate([low, high], axis=dim)


def hbm(value):
    return pltpu.with_memory_space_constraint(value, pltpu.HBM)


def call(kernel, shapes, *args, specs=None, outs=None, scratch=(), first=()):
    n = len(args)
    specs = specs or [VMEM] * (n - 1)
    args = [args[0]] + [hbm(a) if s is ANY else a for a, s in zip(args[1:], specs)]
    first = [hbm(a) for a in first]

    def body(*refs):
        kernel(*refs[:n], *refs[n + len(first) :])

    return pl.pallas_call(
        body,
        out_shape=[jax.ShapeDtypeStruct(s, t) for s, t in shapes],
        in_specs=[SMEM] + specs + [ANY] * len(first),
        out_specs=outs or [VMEM] * len(shapes),
        scratch_shapes=list(scratch),
        compiler_params=PARAMS,
        cost_estimate=pl.CostEstimate(flops=0, bytes_accessed=0, transcendentals=0),
    )(*args, *first)


def fetch(y_at, x_at, pieces, tokens, sems):
    tok = pieces[0].shape[1]
    for k in range(4):

        @pl.when(y_at == k)
        def _(k=k):
            for side in range(2):
                target = tokens.at[pl.ds(side * tok, tok)]
                pltpu.make_async_copy(pieces[2 * k + side].at[x_at], target, sems.at[side]).start()


def fetched(pieces, tokens, sems):
    tok = pieces[0].shape[1]
    for side in range(2):
        target = tokens.at[pl.ds(side * tok, tok)]
        pltpu.make_async_copy(pieces[side].at[0], target, sems.at[side]).wait()


def far_kernel(index, *refs):
    pieces, (weight, up, down, tokens, sems) = refs[:8], refs[8:]
    fetch(index[0], index[1], pieces, tokens, sems)
    fetched(pieces, tokens, sems)
    rows = up.shape[0]
    part = dot(tokens[...], weight[...], (1, 1)).astype(BF16)
    up[...] = part[:rows]
    down[...] = part[rows:]


def part_kernel(index, *refs):
    pieces, weight, outs, (tokens, sems) = refs[:8], refs[8], refs[9:13], refs[13:]
    for k in range(7):
        fetch(index[2 * k], index[2 * k + 1], pieces, tokens.at[k], sems.at[k])
    for k in range(7):
        fetched(pieces, tokens.at[k], sems.at[k])
        outs[k // 2][k % 2] = dot(tokens[k], weight[...], (1, 1))


def grad_kernel(index, *refs):
    acts, pieces, (out, rows, tokens, total, row_sems, sems) = refs[:8], refs[8:16], refs[16:]
    copies = []
    for k in range(8):
        copies.append(pltpu.make_async_copy(acts[k], rows.at[k], row_sems.at[k]))
        copies[k].start()
        fetch(index[2 * k], index[2 * k + 1], pieces, tokens.at[k], sems.at[k])
    for k in range(8):
        copies[k].wait()
        fetched(pieces, tokens.at[k], sems.at[k])
        product = dot(rows[k], tokens[k], (0, 0))
        if k == 0:
            total[...] = product
        elif k < 7:
            total[...] += product
        else:
            out[...] = (total[...] + product).astype(BF16)


def weight_kernel(index, own, other, out, sems):
    rows, d = out.shape[0], own.shape[1]
    at = pl.ds(pl.multiple_of(index[0] * rows, rows), rows)
    copies = [
        pltpu.make_async_copy(own.at[at], out.at[:, pl.ds(0, d)], sems.at[0]),
        pltpu.make_async_copy(other.at[pl.ds(0, rows)], out.at[:, pl.ds(d, d)], sems.at[1]),
    ]
    for c in copies:
        c.start()
    for c in copies:
        c.wait()


def own_kernel(index, grad, right_root, left_root, root_other, left_out, right_out, up_out):
    h = index[0]
    d = grad.shape[0]
    scale = 1.0 / (2 * d)
    at = pl.ds(pl.multiple_of(h * d, d), d)
    there = pl.ds(pl.multiple_of((1 - h) * d, d), d)
    left_out[...] = dot(grad[...], grad[...], (1, 1)) * scale
    right_out[...] = dot(grad[:, :d], grad[...], (0, 0)) * scale
    m = (dot(grad[:, :d], right_root[at], (1, 0)) + dot(grad[:, d:], right_root[there], (1, 0))).astype(BF16)
    up_out[:d] = dot(left_root[:, at], m, (1, 0))
    up_out[d:] = dot(root_other[pl.ds(pl.multiple_of((1 + h) * d, d), d)], m, (1, 0))


def other_kernel(index, *refs):
    (grad, other, right_root, left_root, root_other, left_own, right_own, up_own) = refs[:8]
    left_stats, right_stats, left_new, right_new, update = refs[8:13]
    left_in, right_in, left_buf, right_buf, up_buf, sems = refs[13:]
    h = index[0]
    d = grad.shape[0]
    scale = 1.0 / (2 * d)
    at = pl.ds(pl.multiple_of(h * d, d), d)
    there = pl.ds(pl.multiple_of((1 - h) * d, d), d)
    copy = pltpu.make_async_copy
    ins = [copy(left_stats, left_in, sems.at[0]), copy(right_stats, right_in, sems.at[1])]
    outs = [
        copy(up_buf, update, sems.at[2]),
        copy(left_buf, left_new, sems.at[3]),
        copy(right_buf, right_new, sems.at[4]),
    ]
    for c in ins:
        c.start()
    m = dot(other[:, d:], right_root[at], (1, 0)) + dot(other[:, :d], right_root[there], (1, 0))
    m = m.astype(BF16)
    up_buf[at] = (up_own[:d] + dot(left_root[:, there], m, (1, 0))).astype(BF16)
    part = up_own[d:] + dot(root_other[pl.ds(pl.multiple_of((2 - h) * d, d), d)], m, (1, 0))
    up_buf[there] = part.astype(BF16)
    outs[0].start()
    gram = dot(grad[:, :d], other[:, d:], (1, 1)) + dot(grad[:, d:], other[:, :d], (1, 1))
    ins[0].wait()
    left_buf[:, at] = left_in[:, at] + left_own[...]
    left_buf[:, there] = left_in[:, there] + gram * scale
    outs[1].start()
    mine = other[:, d:]
    gram = dot(mine, other[:, d:], (0, 0))
    ins[1].wait()
    right_buf[:, at] = right_in[:, at] + right_own[:, :d] + gram * scale
    gram = dot(mine, other[:, :d], (0, 0))
    right_buf[:, there] = right_in[:, there] + right_own[:, d:] + gram * scale
    outs[2].start()
    for c in outs:
        c.wait()


def cot_kernel(index, own, pair, far, cross_block, out):
    tok, d = own.shape
    out[0, :, :d] = own[...]
    out[0, :, d:] = pair[tok:]
    out[1, :, :d] = far[...]
    out[1, :, d:] = cross_block[...]


def add_kernel(index, part, up, down, up_out, down_out):
    if up.shape == up_out.shape:
        up_out[...] = (part[0] + up[...].astype(F32)).astype(BF16)
        down_out[...] = (part[1] + down[...].astype(F32)).astype(BF16)
    else:
        rows = up.shape[0]
        up_out[:rows] = (part[0, :rows] + up[...].astype(F32)).astype(BF16)
        up_out[rows:] = part[0, rows:].astype(BF16)
        down_out[:rows] = part[1, :rows].astype(BF16)
        down_out[rows:] = (part[1, rows:] + down[...].astype(F32)).astype(BF16)


def last_kernel(index, part, up, down, keep, send):
    rows = keep.shape[0]

    def total(k):
        at = pl.ds(pl.multiple_of(k * rows, rows), rows)
        return part[0, at] + up[at].astype(F32) + down[at].astype(F32)

    keep[...] = total(index[0]).astype(BF16)
    send[...] = total(1 - index[0]).astype(BF16)


def local(cotangent, activations, down_weight, left_stats, right_stats, left_root, right_root):
    z = lax.axis_index("z")
    h = lax.axis_index("xl")
    xh = lax.axis_index("xh")
    y = lax.axis_index("y")
    core = lax.axis_index("core")
    tok, d = cotangent.shape
    block = left_root.shape[2]
    left_stats, right_stats, left_root, right_root = (
        v[0] for v in (left_stats, right_stats, left_root, right_root)
    )

    nothing = jnp.zeros((1,), jnp.int32)
    sem = pltpu.SemaphoreType.DMA

    both = swap(jnp.concatenate([half(activations, 1 - h, 1), cotangent], 0), "xl")
    cot_cross = cross(cotangent)
    cot_far = swap(cotangent, "xh")
    act = order(h ^ core, half(activations, h, 1), both[:tok], 0)
    near = jnp.concatenate([cotangent, both[tok:]], 1)
    far = jnp.concatenate([cot_far, cot_cross], 1)

    up_1, down_1 = shift(act, "z", 1), shift(act, "z", -1)
    up_2, down_2 = shift(up_1, "z", 1), shift(down_1, "z", -1)
    up_3, down_3 = shift(up_2, "z", 1), shift(down_2, "z", -1)
    up_4 = shift(up_3, "z", 1)

    cot = jnp.stack([near, far])
    cot_s = swap(cot, "core")
    y_up, y_down = shift(cot, "y", 1), shift(cot, "y", -1)
    s_up, s_down = swap(y_up, "core"), swap(y_down, "core")
    y_2 = jnp.stack([shift(y_up[0], "y", 1), shift(y_down[1], "y", -1)])
    s_2 = swap(y_2, "core")
    pieces = (cot, cot_s, y_up, s_up, y_down, s_down, y_2, s_2)

    send = after(half(down_weight, 1 - h, 0), cot)
    weight_root = swap(jnp.concatenate([send, left_root[:, :d], left_root[:, d:]], 0), "xl")
    weight = call(
        weight_kernel,
        [((d, 2 * d), BF16)],
        h[None],
        down_weight,
        weight_root,
        specs=[ANY] * 2,
        scratch=[sem((2,))],
    )[0]

    def places(*ks):
        out = []
        for k in ks:
            target = (z + k) % 8
            offset = (target % 4 - y) % 4
            out += [jnp.where(offset % 2 == 0, offset // 2 * 3, (offset % 4 == 1) + 1), xh ^ (target // 4)]
        return jnp.stack(out)

    grad = call(
        grad_kernel,
        [((d, 2 * d), BF16)],
        places(0, -1, -2, -3, 1, 2, 3, 4),
        act, up_1, up_2, up_3, down_1, down_2, down_3, up_4,
        *pieces,
        specs=[ANY] * 16,
        scratch=[
            pltpu.VMEM((8, 2 * tok, d), BF16),
            pltpu.VMEM((8, 2 * tok, 2 * d), BF16),
            pltpu.VMEM((d, 2 * d), F32),
            sem((8,)),
            sem((8, 2)),
        ],
    )[0]
    other = swap(grad, "xl")

    small, full = ((tok, d), BF16), ((2 * tok, d), BF16)
    up, down = call(
        far_kernel,
        [small, small],
        places(4),
        *pieces,
        weight,
        specs=[ANY] * 8 + [VMEM],
        scratch=[pltpu.VMEM((2 * tok, 2 * d), BF16), sem((2,))],
        first=[up_3, down_3],
    )
    *parts, part_0 = call(
        part_kernel,
        [((2, 2 * tok, d), F32)] * 3 + [((1, 2 * tok, d), F32)],
        places(3, -3, 2, -2, 1, -1, 0),
        *pieces,
        weight,
        specs=[ANY] * 8 + [VMEM],
        scratch=[pltpu.VMEM((7, 2 * tok, 2 * d), BF16), sem((7, 2))],
    )
    up, down = shift(up, "z", 1), shift(down, "z", -1)
    for k, part in enumerate(parts):
        up, down = call(add_kernel, [full, full], nothing, part, up, down)
        up, down = shift(up, "z", 1), shift(down, "z", -1)
    keep, send = call(last_kernel, [small, small], (h ^ core)[None], part_0, up, down)
    input_grad = order(h, keep, swap(send, "xl"), 1)

    left_own, right_own, up_own = call(
        own_kernel,
        [((d, d), F32), ((d, 2 * d), F32), ((2 * d, d), F32)],
        h[None],
        grad,
        right_root,
        left_root,
        weight_root,
    )
    stats = ((d, 2 * d), F32)
    left_new, right_new, update = call(
        other_kernel,
        [stats, stats, ((2 * d, d), BF16)],
        h[None],
        grad,
        other,
        right_root,
        left_root,
        weight_root,
        left_own,
        right_own,
        up_own,
        left_stats,
        right_stats,
        specs=[VMEM] * 8 + [ANY] * 2,
        outs=[ANY] * 3,
        scratch=[pltpu.VMEM((d, 2 * d), F32)] * 4 + [pltpu.VMEM((2 * d, d), BF16), sem((5,))],
    )
    return input_grad, update, left_new[None], right_new[None]


def solution(mesh):
    fine = Mesh(mesh.devices.reshape(8, 2, 2, 4, 2), ("z", "xl", "xh", "y", "core"))
    row, col = ("z", "xl"), ("xh", "y", "core")
    in_specs = (
        P(col, row),
        P(row, col),
        P(col, row),
        P(col, row, None),
        P(col, row, None),
        P(col, row, None),
        P(col, None, row),
    )
    out_specs = (P(row, col), P(col, row), P(col, row, None), P(col, row, None))
    return jax.shard_map(local, mesh=fine, in_specs=in_specs, out_specs=out_specs, check_vma=False)
```

```python
import jax
import jax.numpy as jnp
from jax import lax
from jax.experimental import pallas as pl
from jax.experimental.pallas import tpu as pltpu
from jax.sharding import Mesh, PartitionSpec as P

F32 = jnp.float32
BF16 = jnp.bfloat16
VMEM = pl.BlockSpec(memory_space=pltpu.VMEM)
SMEM = pl.BlockSpec(memory_space=pltpu.SMEM)
ANY = pl.BlockSpec(memory_space=pl.ANY)
PARAMS = pltpu.CompilerParams(vmem_limit_bytes=40 * 1024 * 1024)


def after(value, *others):
    return lax.optimization_barrier((value, *others))[0]


def swap(value, axis):
    return lax.ppermute(value, axis, [(0, 1), (1, 0)])


def shift(value, axis, distance):
    n = lax.axis_size(axis)
    return lax.ppermute(value, axis, [(i, (i + distance) % n) for i in range(n)])


def cross(value):
    return lax.ppermute(value, ("xl", "xh"), [(0, 3), (3, 0), (1, 2), (2, 1)])


def half(value, index, dim):
    size = value.shape[dim] // 2
    return lax.dynamic_slice_in_dim(value, index * size, size, dim)


def dot(a, b, contract):
    return lax.dot_general(a, b, ((contract[:1], contract[1:]), ((), ())), preferred_element_type=F32)


def order(h, own, other, dim):
    low = jnp.where(h == 0, own, other)
    high = jnp.where(h == 0, other, own)
    return jnp.concatenate([low, high], axis=dim)


def hbm(value):
    return pltpu.with_memory_space_constraint(value, pltpu.HBM)


def call(kernel, shapes, *args, specs=None, outs=None, scratch=(), first=()):
    n = len(args)
    specs = specs or [VMEM] * (n - 1)
    args = [args[0]] + [hbm(a) if s is ANY else a for a, s in zip(args[1:], specs)]

    def body(*refs):
        kernel(*refs[:n], *refs[n + len(first) :])

    return pl.pallas_call(
        body,
        out_shape=[jax.ShapeDtypeStruct(s, t) for s, t in shapes],
        in_specs=[SMEM] + specs + [ANY] * len(first),
        out_specs=outs or [VMEM] * len(shapes),
        scratch_shapes=list(scratch),
        compiler_params=PARAMS,
        cost_estimate=pl.CostEstimate(flops=0, bytes_accessed=0, transcendentals=0),
    )(*args, *first)


def fetch(y_at, x_at, pieces, tokens, sems):
    tok = pieces[0].shape[1]
    for k in range(4):

        @pl.when(y_at == k)
        def _(k=k):
            for side in range(2):
                target = tokens.at[pl.ds(side * tok, tok)]
                pltpu.make_async_copy(pieces[2 * k + side].at[x_at], target, sems.at[side]).start()


def fetched(pieces, tokens, sems):
    tok = pieces[0].shape[1]
    for side in range(2):
        target = tokens.at[pl.ds(side * tok, tok)]
        pltpu.make_async_copy(pieces[side].at[0], target, sems.at[side]).wait()


def part_kernel(index, *refs):
    pieces, weight, up, down, outs, (tokens, sems) = refs[:8], refs[8], refs[9], refs[10], refs[11:15], refs[15:]
    for k in range(8):
        fetch(index[2 * k], index[2 * k + 1], pieces, tokens.at[k], sems.at[k])
    for k in range(8):
        fetched(pieces, tokens.at[k], sems.at[k])
        part = dot(tokens[k], weight[...], (1, 1))
        if k == 0:
            rows = up.shape[0]
            up[...] = part[:rows].astype(BF16)
            down[...] = part[rows:].astype(BF16)
        else:
            outs[(k - 1) // 2][(k - 1) % 2] = part


def grad_kernel(index, *refs):
    acts, pieces, (out, rows, tokens, total, row_sems, sems) = refs[:8], refs[8:16], refs[16:]
    copies = []
    for k in range(8):
        copies.append(pltpu.make_async_copy(acts[k], rows.at[k], row_sems.at[k]))
        copies[k].start()
        fetch(index[2 * k], index[2 * k + 1], pieces, tokens.at[k], sems.at[k])
    for k in range(8):
        copies[k].wait()
        fetched(pieces, tokens.at[k], sems.at[k])
        product = dot(rows[k], tokens[k], (0, 0))
        if k == 0:
            total[...] = product
        elif k < 7:
            total[...] += product
        else:
            out[...] = (total[...] + product).astype(BF16)


def weight_kernel(index, own, other, out, sems):
    rows, d = out.shape[0], own.shape[1]
    at = pl.ds(pl.multiple_of(index[0] * rows, rows), rows)
    copies = [
        pltpu.make_async_copy(own.at[at], out.at[:, pl.ds(0, d)], sems.at[0]),
        pltpu.make_async_copy(other.at[pl.ds(0, rows)], out.at[:, pl.ds(d, d)], sems.at[1]),
    ]
    for c in copies:
        c.start()
    for c in copies:
        c.wait()


def own_kernel(index, grad, right_root, left_root, root_other, left_out, right_out, up_out):
    h = index[0]
    d = grad.shape[0]
    scale = 1.0 / (2 * d)
    at = pl.ds(pl.multiple_of(h * d, d), d)
    there = pl.ds(pl.multiple_of((1 - h) * d, d), d)
    left_out[...] = dot(grad[...], grad[...], (1, 1)) * scale
    right_out[...] = dot(grad[:, :d], grad[...], (0, 0)) * scale
    m = (dot(grad[:, :d], right_root[at], (1, 0)) + dot(grad[:, d:], right_root[there], (1, 0))).astype(BF16)
    up_out[:d] = dot(left_root[:, at], m, (1, 0))
    up_out[d:] = dot(root_other[:, at], m, (1, 0))


def other_kernel(index, *refs):
    (grad, other, right_root, left_root, root_other, left_own, right_own, up_own) = refs[:8]
    left_stats, right_stats, left_new, right_new, update = refs[8:13]
    left_in, right_in, left_buf, right_buf, up_buf, sems = refs[13:]
    h = index[0]
    d = grad.shape[0]
    scale = 1.0 / (2 * d)
    at = pl.ds(pl.multiple_of(h * d, d), d)
    there = pl.ds(pl.multiple_of((1 - h) * d, d), d)
    copy = pltpu.make_async_copy
    ins = [copy(left_stats, left_in, sems.at[0]), copy(right_stats, right_in, sems.at[1])]
    outs = [
        copy(up_buf, update, sems.at[2]),
        copy(left_buf, left_new, sems.at[3]),
        copy(right_buf, right_new, sems.at[4]),
    ]
    for c in ins:
        c.start()
    m = dot(other[:, d:], right_root[at], (1, 0)) + dot(other[:, :d], right_root[there], (1, 0))
    m = m.astype(BF16)
    up_buf[at] = (up_own[:d] + dot(left_root[:, there], m, (1, 0))).astype(BF16)
    part = up_own[d:] + dot(root_other[:, there], m, (1, 0))
    up_buf[there] = part.astype(BF16)
    outs[0].start()
    gram = dot(grad[:, :d], other[:, d:], (1, 1)) + dot(grad[:, d:], other[:, :d], (1, 1))
    ins[0].wait()
    left_buf[:, at] = left_in[:, at] + left_own[...]
    left_buf[:, there] = left_in[:, there] + gram * scale
    outs[1].start()
    mine = other[:, d:]
    gram = dot(mine, other[:, d:], (0, 0))
    ins[1].wait()
    right_buf[:, at] = right_in[:, at] + right_own[:, :d] + gram * scale
    gram = dot(mine, other[:, :d], (0, 0))
    right_buf[:, there] = right_in[:, there] + right_own[:, d:] + gram * scale
    outs[2].start()
    for c in outs:
        c.wait()


def cot_kernel(index, own, pair, far, cross_block, out):
    tok, d = own.shape
    out[0, :, :d] = own[...]
    out[0, :, d:] = pair[tok:]
    out[1, :, :d] = far[...]
    out[1, :, d:] = cross_block[...]


def add_kernel(index, part, up, down, up_out, down_out):
    if up.shape == up_out.shape:
        up_out[...] = (part[0] + up[...].astype(F32)).astype(BF16)
        down_out[...] = (part[1] + down[...].astype(F32)).astype(BF16)
    else:
        rows = up.shape[0]
        up_out[:rows] = (part[0, :rows] + up[...].astype(F32)).astype(BF16)
        up_out[rows:] = part[0, rows:].astype(BF16)
        down_out[:rows] = part[1, :rows].astype(BF16)
        down_out[rows:] = (part[1, rows:] + down[...].astype(F32)).astype(BF16)


def last_kernel(index, part, up, down, keep, send):
    rows = keep.shape[0]

    def total(k):
        at = pl.ds(pl.multiple_of(k * rows, rows), rows)
        return part[0, at] + up[at].astype(F32) + down[at].astype(F32)

    keep[...] = total(index[0]).astype(BF16)
    send[...] = total(1 - index[0]).astype(BF16)


def local(cotangent, activations, down_weight, left_stats, right_stats, left_root, right_root):
    z = lax.axis_index("z")
    h = lax.axis_index("xl")
    xh = lax.axis_index("xh")
    y = lax.axis_index("y")
    core = lax.axis_index("core")
    tok, d = cotangent.shape
    block = left_root.shape[2]
    left_stats, right_stats, left_root, right_root = (
        v[0] for v in (left_stats, right_stats, left_root, right_root)
    )

    nothing = jnp.zeros((1,), jnp.int32)
    sem = pltpu.SemaphoreType.DMA

    both = swap(jnp.concatenate([half(activations, 1 - h, 1), cotangent], 0), "xl")
    cot_cross = cross(cotangent)
    cot_far = swap(cotangent, "xh")
    act = order(h ^ core, half(activations, h, 1), both[:tok], 0)
    near = jnp.concatenate([cotangent, both[tok:]], 1)
    far = jnp.concatenate([cot_far, cot_cross], 1)

    up_1, down_1 = shift(act, "z", 1), shift(act, "z", -1)
    up_2, down_2 = shift(up_1, "z", 1), shift(down_1, "z", -1)
    up_3, down_3 = shift(up_2, "z", 1), shift(down_2, "z", -1)
    up_4 = shift(up_3, "z", 1)

    cot = jnp.stack([near, far])
    cot_s = swap(cot, "core")
    y_up, y_down = shift(cot, "y", 1), shift(cot, "y", -1)
    s_up, s_down = swap(y_up, "core"), swap(y_down, "core")
    y_2 = jnp.stack([shift(y_up[0], "y", 1), shift(y_down[1], "y", -1)])
    s_2 = swap(y_2, "core")
    pieces = (cot, cot_s, y_up, s_up, y_down, s_down, y_2, s_2)

    weight_other = swap(after(half(down_weight, 1 - h, 0), cot), "xl")
    root_other = swap(after(left_root, weight_other), "xl")
    weight = call(
        weight_kernel,
        [((d, 2 * d), BF16)],
        h[None],
        down_weight,
        weight_other,
        specs=[ANY] * 2,
        scratch=[sem((2,))],
    )[0]

    def places(*ks):
        out = []
        for k in ks:
            target = (z + k) % 8
            offset = (target % 4 - y) % 4
            out += [jnp.where(offset % 2 == 0, offset // 2 * 3, (offset % 4 == 1) + 1), xh ^ (target // 4)]
        return jnp.stack(out)

    small, full = ((tok, d), BF16), ((2 * tok, d), BF16)
    up, down, *parts, part_0 = call(
        part_kernel,
        [small, small] + [((2, 2 * tok, d), F32)] * 3 + [((1, 2 * tok, d), F32)],
        places(4, 3, -3, 2, -2, 1, -1, 0),
        *pieces,
        weight,
        specs=[ANY] * 8 + [VMEM],
        scratch=[pltpu.VMEM((8, 2 * tok, 2 * d), BF16), sem((8, 2))],
        first=[up_3, down_3],
    )

    grad = call(
        grad_kernel,
        [((d, 2 * d), BF16)],
        places(0, -1, -2, -3, 1, 2, 3, 4),
        act, up_1, up_2, up_3, down_1, down_2, down_3, up_4,
        *pieces,
        specs=[ANY] * 16,
        scratch=[
            pltpu.VMEM((8, 2 * tok, d), BF16),
            pltpu.VMEM((8, 2 * tok, 2 * d), BF16),
            pltpu.VMEM((d, 2 * d), F32),
            sem((8,)),
            sem((8, 2)),
        ],
        first=[up],
    )[0]
    other = swap(grad, "xl")

    left_own, right_own, up_own = call(
        own_kernel,
        [((d, d), F32), ((d, 2 * d), F32), ((2 * d, d), F32)],
        h[None],
        grad,
        right_root,
        left_root,
        root_other,
    )
    up, down = shift(up, "z", 1), shift(down, "z", -1)
    for k, part in enumerate(parts):
        up, down = call(add_kernel, [full, full], nothing, part, up, down, first=[left_own] if k == 1 else [])
        up, down = shift(up, "z", 1), shift(down, "z", -1)
    stats = ((d, 2 * d), F32)
    left_new, right_new, update = call(
        other_kernel,
        [stats, stats, ((2 * d, d), BF16)],
        h[None],
        grad,
        other,
        right_root,
        left_root,
        root_other,
        left_own,
        right_own,
        up_own,
        left_stats,
        right_stats,
        specs=[VMEM] * 8 + [ANY] * 2,
        outs=[ANY] * 3,
        scratch=[pltpu.VMEM((d, 2 * d), F32)] * 4 + [pltpu.VMEM((2 * d, d), BF16), sem((5,))],
    )
    keep, send = call(last_kernel, [small, small], (h ^ core)[None], part_0, up, down, first=[update])
    input_grad = order(h, keep, swap(send, "xl"), 1)

    return input_grad, update, left_new[None], right_new[None]


def solution(mesh):
    fine = Mesh(mesh.devices.reshape(8, 2, 2, 4, 2), ("z", "xl", "xh", "y", "core"))
    row, col = ("z", "xl"), ("xh", "y", "core")
    in_specs = (
        P(col, row),
        P(row, col),
        P(col, row),
        P(col, row, None),
        P(col, row, None),
        P(col, row, None),
        P(col, None, row),
    )
    out_specs = (P(row, col), P(col, row), P(col, row, None), P(col, row, None))
    return jax.shard_map(local, mesh=fine, in_specs=in_specs, out_specs=out_specs, check_vma=False)
```

```python
import jax
import jax.numpy as jnp
from jax import lax
from jax.experimental import pallas as pl
from jax.experimental.pallas import tpu as pltpu
from jax.sharding import Mesh, PartitionSpec as P

F32 = jnp.float32
BF16 = jnp.bfloat16
VMEM = pl.BlockSpec(memory_space=pltpu.VMEM)
SMEM = pl.BlockSpec(memory_space=pltpu.SMEM)
ANY = pl.BlockSpec(memory_space=pl.ANY)
PARAMS = pltpu.CompilerParams(vmem_limit_bytes=40 * 1024 * 1024)


def after(value, *others):
    return lax.optimization_barrier((value, *others))[0]


def swap(value, axis):
    return lax.ppermute(value, axis, [(0, 1), (1, 0)])


def shift(value, axis, distance):
    n = lax.axis_size(axis)
    return lax.ppermute(value, axis, [(i, (i + distance) % n) for i in range(n)])


def cross(value):
    return lax.ppermute(value, ("xl", "xh"), [(0, 3), (3, 0), (1, 2), (2, 1)])


def half(value, index, dim):
    size = value.shape[dim] // 2
    return lax.dynamic_slice_in_dim(value, index * size, size, dim)


def dot(a, b, contract):
    return lax.dot_general(a, b, ((contract[:1], contract[1:]), ((), ())), preferred_element_type=F32)


def order(h, own, other, dim):
    low = jnp.where(h == 0, own, other)
    high = jnp.where(h == 0, other, own)
    return jnp.concatenate([low, high], axis=dim)


def hbm(value):
    return pltpu.with_memory_space_constraint(value, pltpu.HBM)


def call(kernel, shapes, *args, specs=None, outs=None, scratch=(), first=()):
    n = len(args)
    specs = specs or [VMEM] * (n - 1)
    args = [args[0]] + [hbm(a) if s is ANY else a for a, s in zip(args[1:], specs)]

    def body(*refs):
        kernel(*refs[:n], *refs[n + len(first) :])

    return pl.pallas_call(
        body,
        out_shape=[jax.ShapeDtypeStruct(s, t) for s, t in shapes],
        in_specs=[SMEM] + specs + [ANY] * len(first),
        out_specs=outs or [VMEM] * len(shapes),
        scratch_shapes=list(scratch),
        compiler_params=PARAMS,
        cost_estimate=pl.CostEstimate(flops=0, bytes_accessed=0, transcendentals=0),
    )(*args, *first)


def block(k):
    return pl.ds(pl.multiple_of(k * 256, 256), 256)


def fetch(pieces, tokens, sems):
    tok = pieces[0].shape[1]
    copies = []
    for k, piece in enumerate(pieces):
        for i in range(2):
            at = pl.ds((k // 2 * 2 + i) * 2 * tok + k % 2 * tok, tok)
            copies.append(pltpu.make_async_copy(piece.at[i], tokens.at[at], sems.at[2 * k + i]))
            copies[-1].start()
    return copies


def part_kernel(index, *refs):
    pieces, weight, up, down, outs, (tokens, sems) = refs[:8], refs[8], refs[9], refs[10], refs[11:15], refs[15:]
    for c in fetch(pieces, tokens, sems):
        c.wait()
    for k in range(8):
        part = dot(tokens[block(2 * index[2 * k] + index[2 * k + 1])], weight[...], (1, 1))
        if k == 0:
            rows = up.shape[0]
            up[...] = part[:rows].astype(BF16)
            down[...] = part[rows:].astype(BF16)
        else:
            outs[(k - 1) // 2][(k - 1) % 2] = part


def grad_kernel(index, *refs):
    acts, pieces, (out, rows, tokens, total, row_sems, sems) = refs[:8], refs[8:16], refs[16:]
    copies = []
    for k in range(8):
        at = block(2 * index[2 * k] + index[2 * k + 1])
        copies.append(pltpu.make_async_copy(acts[k], rows.at[at], row_sems.at[k]))
        copies[-1].start()
    copies += fetch(pieces, tokens, sems)
    for c in copies:
        c.wait()
    out[...] = dot(rows[...], tokens[...], (0, 0)).astype(BF16)


def send_kernel(index, act, own, out, sems):
    tok, d = own.shape
    at = pl.ds(pl.multiple_of(index[0] * d, d), d)
    copies = [
        pltpu.make_async_copy(act.at[:, at], out.at[pl.ds(0, tok)], sems.at[0]),
        pltpu.make_async_copy(own, out.at[pl.ds(tok, tok)], sems.at[1]),
    ]
    for c in copies:
        c.start()
    for c in copies:
        c.wait()


def weight_kernel(index, own, other, out, sems):
    rows, d = out.shape[0], own.shape[1]
    at = pl.ds(pl.multiple_of(index[0] * rows, rows), rows)
    copies = [
        pltpu.make_async_copy(own.at[at], out.at[:, pl.ds(0, d)], sems.at[0]),
        pltpu.make_async_copy(other.at[pl.ds(0, rows)], out.at[:, pl.ds(d, d)], sems.at[1]),
    ]
    for c in copies:
        c.start()
    for c in copies:
        c.wait()


def own_kernel(index, grad, right_root, left_root, root_other, left_out, right_out, up_out):
    h = index[0]
    d = grad.shape[0]
    scale = 1.0 / (2 * d)
    at = pl.ds(pl.multiple_of(h * d, d), d)
    there = pl.ds(pl.multiple_of((1 - h) * d, d), d)
    left_out[...] = dot(grad[...], grad[...], (1, 1)) * scale
    right_out[...] = dot(grad[:, :d], grad[...], (0, 0)) * scale
    m = (dot(grad[:, :d], right_root[at], (1, 0)) + dot(grad[:, d:], right_root[there], (1, 0))).astype(BF16)
    up_out[:d] = dot(left_root[:, at], m, (1, 0))
    up_out[d:] = dot(root_other[:, at], m, (1, 0))


def other_kernel(index, *refs):
    (grad, other, right_root, left_root, root_other, left_own, right_own, up_own) = refs[:8]
    left_stats, right_stats, left_new, right_new, update = refs[8:13]
    left_in, right_in, left_buf, right_buf, up_buf, sems = refs[13:]
    h = index[0]
    d = grad.shape[0]
    scale = 1.0 / (2 * d)
    at = pl.ds(pl.multiple_of(h * d, d), d)
    there = pl.ds(pl.multiple_of((1 - h) * d, d), d)
    copy = pltpu.make_async_copy
    ins = [copy(left_stats, left_in, sems.at[0]), copy(right_stats, right_in, sems.at[1])]
    outs = [
        copy(up_buf, update, sems.at[2]),
        copy(left_buf, left_new, sems.at[3]),
        copy(right_buf, right_new, sems.at[4]),
    ]
    for c in ins:
        c.start()
    m = dot(other[:, d:], right_root[at], (1, 0)) + dot(other[:, :d], right_root[there], (1, 0))
    m = m.astype(BF16)
    up_buf[at] = (up_own[:d] + dot(left_root[:, there], m, (1, 0))).astype(BF16)
    part = up_own[d:] + dot(root_other[:, there], m, (1, 0))
    up_buf[there] = part.astype(BF16)
    outs[0].start()
    gram = dot(grad[:, :d], other[:, d:], (1, 1)) + dot(grad[:, d:], other[:, :d], (1, 1))
    ins[0].wait()
    left_buf[:, at] = left_in[:, at] + left_own[...]
    left_buf[:, there] = left_in[:, there] + gram * scale
    outs[1].start()
    mine = other[:, d:]
    gram = dot(mine, other[:, d:], (0, 0))
    ins[1].wait()
    right_buf[:, at] = right_in[:, at] + right_own[:, :d] + gram * scale
    gram = dot(mine, other[:, :d], (0, 0))
    right_buf[:, there] = right_in[:, there] + right_own[:, d:] + gram * scale
    outs[2].start()
    for c in outs:
        c.wait()


def cot_kernel(index, own, pair, far, cross_block, out):
    tok, d = own.shape
    out[0, :, :d] = own[...]
    out[0, :, d:] = pair[tok:]
    out[1, :, :d] = far[...]
    out[1, :, d:] = cross_block[...]


def add_kernel(index, part, up, down, up_out, down_out):
    if up.shape == up_out.shape:
        up_out[...] = (part[0] + up[...].astype(F32)).astype(BF16)
        down_out[...] = (part[1] + down[...].astype(F32)).astype(BF16)
    else:
        rows = up.shape[0]
        up_out[:rows] = (part[0, :rows] + up[...].astype(F32)).astype(BF16)
        up_out[rows:] = part[0, rows:].astype(BF16)
        down_out[:rows] = part[1, :rows].astype(BF16)
        down_out[rows:] = (part[1, rows:] + down[...].astype(F32)).astype(BF16)


def last_kernel(index, part, up, down, keep, send):
    rows = keep.shape[0]

    def total(k):
        at = pl.ds(pl.multiple_of(k * rows, rows), rows)
        return part[0, at] + up[at].astype(F32) + down[at].astype(F32)

    keep[...] = total(index[0]).astype(BF16)
    send[...] = total(1 - index[0]).astype(BF16)


def local(cotangent, activations, down_weight, left_stats, right_stats, left_root, right_root):
    z = lax.axis_index("z")
    h = lax.axis_index("xl")
    xh = lax.axis_index("xh")
    y = lax.axis_index("y")
    core = lax.axis_index("core")
    tok, d = cotangent.shape
    block = left_root.shape[2]
    left_stats, right_stats, left_root, right_root = (
        v[0] for v in (left_stats, right_stats, left_root, right_root)
    )

    nothing = jnp.zeros((1,), jnp.int32)
    sem = pltpu.SemaphoreType.DMA

    both = call(
        send_kernel,
        [((2 * tok, d), BF16)],
        (1 - h)[None],
        activations,
        cotangent,
        specs=[ANY] * 2,
        scratch=[sem((2,))],
    )[0]
    both = swap(both, "xl")
    cot_cross = cross(cotangent)
    cot_far = swap(cotangent, "xh")
    act = order(h ^ core, half(activations, h, 1), both[:tok], 0)
    near = jnp.concatenate([cotangent, both[tok:]], 1)
    far = jnp.concatenate([cot_far, cot_cross], 1)

    up_1, down_1 = shift(act, "z", 1), shift(act, "z", -1)
    up_2, down_2 = shift(up_1, "z", 1), shift(down_1, "z", -1)
    up_3, down_3 = shift(up_2, "z", 1), shift(down_2, "z", -1)
    up_4 = shift(up_3, "z", 1)

    cot = jnp.stack([near, far])
    cot_s = swap(cot, "core")
    y_up, y_down = shift(cot, "y", 1), shift(cot, "y", -1)
    s_up, s_down = swap(y_up, "core"), swap(y_down, "core")
    y_2 = jnp.stack([shift(y_up[0], "y", 1), shift(y_down[1], "y", -1)])
    s_2 = swap(y_2, "core")
    pieces = (cot, cot_s, y_up, s_up, y_down, s_down, y_2, s_2)

    weight_other = swap(after(half(down_weight, 1 - h, 0), cot), "xl")
    root_other = swap(after(left_root, weight_other), "xl")
    weight = call(
        weight_kernel,
        [((d, 2 * d), BF16)],
        h[None],
        down_weight,
        weight_other,
        specs=[ANY] * 2,
        scratch=[sem((2,))],
    )[0]

    def places(*ks):
        out = []
        for k in ks:
            target = (z + k) % 8
            offset = (target % 4 - y) % 4
            out += [jnp.where(offset % 2 == 0, offset // 2 * 3, (offset % 4 == 1) + 1), xh ^ (target // 4)]
        return jnp.stack(out)

    small, full = ((tok, d), BF16), ((2 * tok, d), BF16)
    up, down, *parts, part_0 = call(
        part_kernel,
        [small, small] + [((2, 2 * tok, d), F32)] * 3 + [((1, 2 * tok, d), F32)],
        places(4, 3, -3, 2, -2, 1, -1, 0),
        *pieces,
        weight,
        specs=[ANY] * 8 + [VMEM],
        scratch=[pltpu.VMEM((16 * tok, 2 * d), BF16), sem((16,))],
        first=[up_3, down_3],
    )

    grad = call(
        grad_kernel,
        [((d, 2 * d), BF16)],
        places(0, -1, -2, -3, 1, 2, 3, 4),
        act, up_1, up_2, up_3, down_1, down_2, down_3, up_4,
        *pieces,
        specs=[ANY] * 16,
        scratch=[
            pltpu.VMEM((16 * tok, d), BF16),
            pltpu.VMEM((16 * tok, 2 * d), BF16),
            pltpu.VMEM((d, 2 * d), F32),
            sem((8,)),
            sem((16,)),
        ],
        first=[up],
    )[0]
    other = swap(grad, "xl")

    left_own, right_own, up_own = call(
        own_kernel,
        [((d, d), F32), ((d, 2 * d), F32), ((2 * d, d), F32)],
        h[None],
        grad,
        right_root,
        left_root,
        root_other,
    )
    up, down = shift(up, "z", 1), shift(down, "z", -1)
    for k, part in enumerate(parts):
        up, down = call(add_kernel, [full, full], nothing, part, up, down, first=[left_own] if k == 1 else [])
        up, down = shift(up, "z", 1), shift(down, "z", -1)
    stats = ((d, 2 * d), F32)
    left_new, right_new, update = call(
        other_kernel,
        [stats, stats, ((2 * d, d), BF16)],
        h[None],
        grad,
        other,
        right_root,
        left_root,
        root_other,
        left_own,
        right_own,
        up_own,
        left_stats,
        right_stats,
        specs=[VMEM] * 8 + [ANY] * 2,
        outs=[ANY] * 3,
        scratch=[pltpu.VMEM((d, 2 * d), F32)] * 4 + [pltpu.VMEM((2 * d, d), BF16), sem((5,))],
    )
    keep, send = call(last_kernel, [small, small], (h ^ core)[None], part_0, up, down, first=[hbm(update)])
    input_grad = order(h, keep, swap(send, "xl"), 1)

    return input_grad, update, left_new[None], right_new[None]


def solution(mesh):
    fine = Mesh(mesh.devices.reshape(8, 2, 2, 4, 2), ("z", "xl", "xh", "y", "core"))
    row, col = ("z", "xl"), ("xh", "y", "core")
    in_specs = (
        P(col, row),
        P(row, col),
        P(col, row),
        P(col, row, None),
        P(col, row, None),
        P(col, row, None),
        P(col, None, row),
    )
    out_specs = (P(row, col), P(col, row), P(col, row, None), P(col, row, None))
    return jax.shard_map(local, mesh=fine, in_specs=in_specs, out_specs=out_specs, check_vma=False)
```

```python
import jax
import jax.numpy as jnp
from jax import lax
from jax.experimental import pallas as pl
from jax.experimental.pallas import tpu as pltpu
from jax.sharding import Mesh, PartitionSpec as P

F32 = jnp.float32
BF16 = jnp.bfloat16
VMEM = pl.BlockSpec(memory_space=pltpu.VMEM)
SMEM = pl.BlockSpec(memory_space=pltpu.SMEM)
ANY = pl.BlockSpec(memory_space=pl.ANY)
PARAMS = pltpu.CompilerParams(vmem_limit_bytes=40 * 1024 * 1024)


def after(value, *others):
    return lax.optimization_barrier((value, *others))[0]


def swap(value, axis):
    return lax.ppermute(value, axis, [(0, 1), (1, 0)])


def shift(value, axis, distance):
    n = lax.axis_size(axis)
    return lax.ppermute(value, axis, [(i, (i + distance) % n) for i in range(n)])


def cross(value):
    return lax.ppermute(value, ("xl", "xh"), [(0, 3), (3, 0), (1, 2), (2, 1)])


def half(value, index, dim):
    size = value.shape[dim] // 2
    return lax.dynamic_slice_in_dim(value, index * size, size, dim)


def dot(a, b, contract):
    return lax.dot_general(a, b, ((contract[:1], contract[1:]), ((), ())), preferred_element_type=F32)


def order(h, own, other, dim):
    low = jnp.where(h == 0, own, other)
    high = jnp.where(h == 0, other, own)
    return jnp.concatenate([low, high], axis=dim)


def hbm(value):
    return pltpu.with_memory_space_constraint(value, pltpu.HBM)


def call(kernel, shapes, *args, specs=None, outs=None, scratch=(), first=()):
    n = len(args)
    specs = specs or [VMEM] * (n - 1)
    args = [args[0]] + [hbm(a) if s is ANY else a for a, s in zip(args[1:], specs)]

    def body(*refs):
        kernel(*refs[:n], *refs[n + len(first) :])

    return pl.pallas_call(
        body,
        out_shape=[jax.ShapeDtypeStruct(s, t) for s, t in shapes],
        in_specs=[SMEM] + specs + [ANY] * len(first),
        out_specs=outs or [VMEM] * len(shapes),
        scratch_shapes=list(scratch),
        compiler_params=PARAMS,
        cost_estimate=pl.CostEstimate(flops=0, bytes_accessed=0, transcendentals=0),
    )(*args, *first)


def block(k):
    return pl.ds(pl.multiple_of(k * 256, 256), 256)


def fetch(pieces, tokens, sems):
    tok = pieces[0].shape[1]
    copies = []
    for k, piece in enumerate(pieces):
        for i in range(2):
            at = pl.ds((k // 2 * 2 + i) * 2 * tok + k % 2 * tok, tok)
            copies.append(pltpu.make_async_copy(piece.at[i], tokens.at[at], sems.at[2 * k + i]))
            copies[-1].start()
    return copies


def part_kernel(index, *refs):
    pieces, weight, up, down, outs, (tokens, sems) = refs[:8], refs[8], refs[9], refs[10], refs[11:15], refs[15:]
    for c in fetch(pieces, tokens, sems):
        c.wait()
    for k in range(8):
        part = dot(tokens[block(2 * index[2 * k] + index[2 * k + 1])], weight[...], (1, 1))
        if k == 0:
            rows = up.shape[0]
            up[...] = part[:rows].astype(BF16)
            down[...] = part[rows:].astype(BF16)
        else:
            outs[(k - 1) // 2][(k - 1) % 2] = part.astype(BF16)


def grad_kernel(index, *refs):
    acts, pieces, (out, rows, tokens, total, row_sems, sems) = refs[:8], refs[8:16], refs[16:]
    copies = []
    for k in range(8):
        at = block(2 * index[2 * k] + index[2 * k + 1])
        copies.append(pltpu.make_async_copy(acts[k], rows.at[at], row_sems.at[k]))
        copies[-1].start()
    copies += fetch(pieces, tokens, sems)
    for c in copies:
        c.wait()
    out[...] = dot(rows[...], tokens[...], (0, 0)).astype(BF16)


def send_kernel(index, act, own, out, sems):
    tok, d = own.shape
    at = pl.ds(pl.multiple_of(index[0] * d, d), d)
    copies = [
        pltpu.make_async_copy(act.at[:, at], out.at[pl.ds(0, tok)], sems.at[0]),
        pltpu.make_async_copy(own, out.at[pl.ds(tok, tok)], sems.at[1]),
    ]
    for c in copies:
        c.start()
    for c in copies:
        c.wait()


def weight_kernel(index, own, other, out, sems):
    rows, d = out.shape[0], own.shape[1]
    at = pl.ds(pl.multiple_of(index[0] * rows, rows), rows)
    copies = [
        pltpu.make_async_copy(own.at[at], out.at[:, pl.ds(0, d)], sems.at[0]),
        pltpu.make_async_copy(other.at[pl.ds(0, rows)], out.at[:, pl.ds(d, d)], sems.at[1]),
    ]
    for c in copies:
        c.start()
    for c in copies:
        c.wait()


def own_kernel(index, grad, right_root, left_root, root_other, left_out, right_out, up_out):
    h = index[0]
    d = grad.shape[0]
    scale = 1.0 / (2 * d)
    at = pl.ds(pl.multiple_of(h * d, d), d)
    there = pl.ds(pl.multiple_of((1 - h) * d, d), d)
    left_out[...] = dot(grad[...], grad[...], (1, 1)) * scale
    right_out[...] = dot(grad[:, :d], grad[...], (0, 0)) * scale
    m = (dot(grad[:, :d], right_root[at], (1, 0)) + dot(grad[:, d:], right_root[there], (1, 0))).astype(BF16)
    up_out[:d] = dot(left_root[:, at], m, (1, 0))
    up_out[d:] = dot(root_other[:, at], m, (1, 0))


def other_kernel(index, *refs):
    (grad, other, right_root, left_root, root_other, left_own, right_own, up_own) = refs[:8]
    left_stats, right_stats, left_new, right_new, update = refs[8:13]
    left_in, right_in, left_buf, right_buf, up_buf, sems = refs[13:]
    h = index[0]
    d = grad.shape[0]
    scale = 1.0 / (2 * d)
    at = pl.ds(pl.multiple_of(h * d, d), d)
    there = pl.ds(pl.multiple_of((1 - h) * d, d), d)
    copy = pltpu.make_async_copy
    ins = [copy(left_stats, left_in, sems.at[0]), copy(right_stats, right_in, sems.at[1])]
    outs = [
        copy(up_buf, update, sems.at[2]),
        copy(left_buf, left_new, sems.at[3]),
        copy(right_buf, right_new, sems.at[4]),
    ]
    for c in ins:
        c.start()
    m = dot(other[:, d:], right_root[at], (1, 0)) + dot(other[:, :d], right_root[there], (1, 0))
    m = m.astype(BF16)
    up_buf[at] = (up_own[:d] + dot(left_root[:, there], m, (1, 0))).astype(BF16)
    part = up_own[d:] + dot(root_other[:, there], m, (1, 0))
    up_buf[there] = part.astype(BF16)
    outs[0].start()
    gram = dot(grad[:, :d], other[:, d:], (1, 1)) + dot(grad[:, d:], other[:, :d], (1, 1))
    ins[0].wait()
    left_buf[:, at] = left_in[:, at] + left_own[...]
    left_buf[:, there] = left_in[:, there] + gram * scale
    outs[1].start()
    mine = other[:, d:]
    gram = dot(mine, other[:, d:], (0, 0))
    ins[1].wait()
    right_buf[:, at] = right_in[:, at] + right_own[:, :d] + gram * scale
    gram = dot(mine, other[:, :d], (0, 0))
    right_buf[:, there] = right_in[:, there] + right_own[:, d:] + gram * scale
    outs[2].start()
    for c in outs:
        c.wait()


def cot_kernel(index, own, pair, far, cross_block, out):
    tok, d = own.shape
    out[0, :, :d] = own[...]
    out[0, :, d:] = pair[tok:]
    out[1, :, :d] = far[...]
    out[1, :, d:] = cross_block[...]


def add_kernel(index, part, up, down, up_out, down_out):
    if up.shape == up_out.shape:
        up_out[...] = (part[0] + up[...].astype(F32)).astype(BF16)
        down_out[...] = (part[1] + down[...].astype(F32)).astype(BF16)
    else:
        rows = up.shape[0]
        up_out[:rows] = (part[0, :rows] + up[...].astype(F32)).astype(BF16)
        up_out[rows:] = part[0, rows:].astype(BF16)
        down_out[:rows] = part[1, :rows].astype(BF16)
        down_out[rows:] = (part[1, rows:] + down[...].astype(F32)).astype(BF16)


def last_kernel(index, part, up, down, keep, send):
    rows = keep.shape[0]

    def total(k):
        at = pl.ds(pl.multiple_of(k * rows, rows), rows)
        return part[0, at] + up[at].astype(F32) + down[at].astype(F32)

    keep[...] = total(index[0]).astype(BF16)
    send[...] = total(1 - index[0]).astype(BF16)


def local(cotangent, activations, down_weight, left_stats, right_stats, left_root, right_root):
    z = lax.axis_index("z")
    h = lax.axis_index("xl")
    xh = lax.axis_index("xh")
    y = lax.axis_index("y")
    core = lax.axis_index("core")
    tok, d = cotangent.shape
    block = left_root.shape[2]
    left_stats, right_stats, left_root, right_root = (
        v[0] for v in (left_stats, right_stats, left_root, right_root)
    )

    nothing = jnp.zeros((1,), jnp.int32)
    sem = pltpu.SemaphoreType.DMA

    both = call(
        send_kernel,
        [((2 * tok, d), BF16)],
        (1 - h)[None],
        activations,
        cotangent,
        specs=[ANY] * 2,
        scratch=[sem((2,))],
    )[0]
    both = swap(both, "xl")
    cot_cross = cross(cotangent)
    cot_far = swap(cotangent, "xh")
    act = order(h ^ core, half(activations, h, 1), both[:tok], 0)
    near = jnp.concatenate([cotangent, both[tok:]], 1)
    far = jnp.concatenate([cot_far, cot_cross], 1)

    up_1, down_1 = shift(act, "z", 1), shift(act, "z", -1)
    up_2, down_2 = shift(up_1, "z", 1), shift(down_1, "z", -1)
    up_3, down_3 = shift(up_2, "z", 1), shift(down_2, "z", -1)
    up_4 = shift(up_3, "z", 1)

    cot = jnp.stack([near, far])
    cot_s = swap(cot, "core")
    y_up, y_down = shift(cot, "y", 1), shift(cot, "y", -1)
    s_up, s_down = swap(y_up, "core"), swap(y_down, "core")
    y_2 = jnp.stack([shift(y_up[0], "y", 1), shift(y_down[1], "y", -1)])
    s_2 = swap(y_2, "core")
    pieces = (cot, cot_s, y_up, s_up, y_down, s_down, y_2, s_2)

    weight_other = swap(after(half(down_weight, 1 - h, 0), cot), "xl")
    root_other = swap(after(left_root, weight_other), "xl")
    weight = call(
        weight_kernel,
        [((d, 2 * d), BF16)],
        h[None],
        down_weight,
        weight_other,
        specs=[ANY] * 2,
        scratch=[sem((2,))],
    )[0]

    def places(*ks):
        out = []
        for k in ks:
            target = (z + k) % 8
            offset = (target % 4 - y) % 4
            out += [jnp.where(offset % 2 == 0, offset // 2 * 3, (offset % 4 == 1) + 1), xh ^ (target // 4)]
        return jnp.stack(out)

    small, full = ((tok, d), BF16), ((2 * tok, d), BF16)
    up, down, *parts, part_0 = call(
        part_kernel,
        [small, small] + [((2, 2 * tok, d), BF16)] * 3 + [((1, 2 * tok, d), BF16)],
        places(4, 3, -3, 2, -2, 1, -1, 0),
        *pieces,
        weight,
        specs=[ANY] * 8 + [VMEM],
        scratch=[pltpu.VMEM((16 * tok, 2 * d), BF16), sem((16,))],
        first=[up_3, down_3],
    )

    grad = call(
        grad_kernel,
        [((d, 2 * d), BF16)],
        places(0, -1, -2, -3, 1, 2, 3, 4),
        act, up_1, up_2, up_3, down_1, down_2, down_3, up_4,
        *pieces,
        specs=[ANY] * 16,
        scratch=[
            pltpu.VMEM((16 * tok, d), BF16),
            pltpu.VMEM((16 * tok, 2 * d), BF16),
            pltpu.VMEM((d, 2 * d), F32),
            sem((8,)),
            sem((16,)),
        ],
        first=[up],
    )[0]
    other = swap(grad, "xl")

    left_own, right_own, up_own = call(
        own_kernel,
        [((d, d), F32), ((d, 2 * d), F32), ((2 * d, d), F32)],
        h[None],
        grad,
        right_root,
        left_root,
        root_other,
    )
    up, down = shift(up, "z", 1), shift(down, "z", -1)
    for k, part in enumerate(parts):
        up, down = call(add_kernel, [full, full], nothing, part, up, down, first=[left_own] if k == 1 else [])
        up, down = shift(up, "z", 1), shift(down, "z", -1)
    stats = ((d, 2 * d), F32)
    left_new, right_new, update = call(
        other_kernel,
        [stats, stats, ((2 * d, d), BF16)],
        h[None],
        grad,
        other,
        right_root,
        left_root,
        root_other,
        left_own,
        right_own,
        up_own,
        left_stats,
        right_stats,
        specs=[VMEM] * 8 + [ANY] * 2,
        outs=[ANY] * 3,
        scratch=[pltpu.VMEM((d, 2 * d), F32)] * 4 + [pltpu.VMEM((2 * d, d), BF16), sem((5,))],
    )
    keep, send = call(last_kernel, [small, small], (h ^ core)[None], part_0, up, down, first=[hbm(update)])
    input_grad = order(h, keep, swap(send, "xl"), 1)

    return input_grad, update, left_new[None], right_new[None]


def solution(mesh):
    fine = Mesh(mesh.devices.reshape(8, 2, 2, 4, 2), ("z", "xl", "xh", "y", "core"))
    row, col = ("z", "xl"), ("xh", "y", "core")
    in_specs = (
        P(col, row),
        P(row, col),
        P(col, row),
        P(col, row, None),
        P(col, row, None),
        P(col, row, None),
        P(col, None, row),
    )
    out_specs = (P(row, col), P(col, row), P(col, row, None), P(col, row, None))
    return jax.shard_map(local, mesh=fine, in_specs=in_specs, out_specs=out_specs, check_vma=False)
```
